256 devices in a mesh: leaf: 8 (over y, core), front: 32 (over z, x).
Axes of the slice: x: 4, y: 4, z: 8, core: 2. Of those that a mesh axis runs over, the one named last changes fastest.
Arguments:
- leaf_inverse: bfloat16 [8192, 128, 128], P(('leaf', 'front')), may hold values from -0.5 to 0.5
- leaf_rhs: bfloat16 [8192, 128, 256], P(('leaf', 'front')), may hold values from -6 to 6
- off_blocks: bfloat16 [8192, 5, 128, 128], P(('leaf', 'front')), may hold values from -0.0546875 to 0.0546875
- block_rows: int32 [8192, 5], P(('leaf', 'front')), may hold values from 0 to 63
- fill_count: int32 [8192], P(('leaf', 'front')), may hold values from 1 to 5
- sep_rhs: bfloat16 [256, 128, 256], P(('leaf', 'front')), may hold values from -6 to 6
- panel_order: int32 [8, 32], P('leaf'), may hold values from 0 to 31, each once within a row
- sep_inverse: bfloat16 [256, 128, 4096], P(('leaf', 'front')), may hold values from -0.09375 to 0.09375
Outputs:
- leaf_solution: bfloat16 [8192, 128, 256], P(('leaf', 'front'))
- sep_forward: bfloat16 [256, 128, 256], P(('leaf', 'front'))
- sep_solution: float32 [256, 128, 256], P(('leaf', 'front'))
The draws below stay inside these ranges and needn't reach their ends.
Inputs may be any that keep to these rules, and one draw needn't show every extreme that they name: Each row of panel_order is a permutation of the 32 separators of that front.
All inputs are finite; a program needn't handle non-finite values.
Results may differ from the reference program's by a relative error of at most 0.025.
Values may be sent and summed in bfloat16 or wider, within the bound.
No kernel may reach another device: no remote copies, remote signals or barrier semaphores. Data moves between devices by JAX's collectives and lax.ppermute only.
A program may use at most 128 MiB of HBM per device.

```python
import jax
import jax.numpy as jnp
from jax import lax

B = 128
R = 256
P_SIZE = 5
K_DEV = 32
SEP_DEV = 1
LEAVES = 8192
SEPS = 32
NSEP = 256
N_LEAF = 8
N_FRONT = 32


def touch_ends(values, stream_key, low, largest):
    longest = values.shape.index(max(values.shape))
    spots = []
    for shift in (0, 1):
        where = [jax.random.randint(jax.random.fold_in(stream_key, axis), (), 0, length) for axis, length in enumerate(values.shape)]
        where[longest] = (where[longest] + shift) % values.shape[longest]
        spots.append(tuple(where))
    return values.at[spots[0]].set(low).at[spots[1]].set(largest)


def block_scale(rng, shape, cuts, smallest, largest):
    gain = 1.0
    for dim, blocks in cuts:
        heights = jax.random.uniform(jax.random.fold_in(jax.random.fold_in(rng, 6), dim), (blocks,), jnp.float32, smallest / len(cuts), largest / len(cuts))
        gain = gain * jnp.repeat(jnp.exp(heights), shape[dim] // blocks).reshape((-1,) + (1,) * (len(shape) - 1 - dim))
    return gain


def scatter_about(stream_key, dims, width, bound, shards=(), kind=jnp.bfloat16):
    factor_of = block_scale(stream_key, dims, shards, -0.22, 0.18) if shards else 1.0
    entries = jax.random.normal(stream_key, dims, jnp.float32) * width * factor_of
    return jnp.minimum(jnp.maximum(entries, -bound), bound).astype(kind)


def setup_inputs(seed: int = 0) -> dict:
    key_of = jax.random.split(jax.random.key(seed), 9)
    return {
        "leaf_inverse": scatter_about(key_of[0], (LEAVES, B, B), B ** -0.5, 0.5, ((0, 256),)),
        "leaf_rhs": scatter_about(key_of[1], (LEAVES, B, R), 1.0, 6.0, ((0, 256),)),
        "off_blocks": scatter_about(key_of[2], (LEAVES, P_SIZE, B, B), (3 * B * K_DEV // SEP_DEV) ** -0.5, 0.0546875, ((0, 256),)),
        "block_rows": touch_ends(jax.random.randint(key_of[3], (LEAVES, P_SIZE), 0, 2 * SEPS), jax.random.fold_in(key_of[3], 1), 0, (2 * SEPS) - 1).astype(jnp.int32),
        "fill_count": touch_ends(jax.random.randint(key_of[4], (LEAVES,), 1, P_SIZE + 1), jax.random.fold_in(key_of[4], 1), 1, P_SIZE).astype(jnp.int32),
        "sep_rhs": scatter_about(key_of[5], (NSEP, B, R), 1.0, 6.0, ((0, 256),)),
        "panel_order": jax.vmap(lambda own: jax.random.permutation(own, SEPS))(jax.random.split(key_of[6], N_LEAF)).reshape((N_LEAF, SEPS)).astype(jnp.int32),
        "sep_inverse": scatter_about(key_of[7], (NSEP, B, SEPS * B), (SEPS * B) ** -0.5, 0.09375, ((0, 256),)),
    }


def forward_leaves(pieces):
    inverse_one, rhs_one = pieces
    return jnp.einsum('kab,kbr->kar', inverse_one.astype(jnp.float32), rhs_one.astype(jnp.float32)).astype(jnp.bfloat16)


def reference(leaf_inverse, leaf_rhs, off_blocks, block_rows, fill_count, sep_rhs, panel_order, sep_inverse):
    devices = N_LEAF * N_FRONT
    front_seps = SEP_DEV * N_FRONT
    inverse_dev = leaf_inverse.reshape(devices, K_DEV, B, B)
    rhs_dev = leaf_rhs.reshape(devices, K_DEV, B, R)
    off_dev = off_blocks.reshape(devices, K_DEV, P_SIZE, B, B)
    rows_dev = block_rows.reshape(devices, K_DEV, P_SIZE)
    fill_dev = fill_count.reshape(devices, K_DEV)
    forward = lax.map(forward_leaves, (inverse_dev, rhs_dev))
    indices = jnp.arange(devices, dtype=jnp.int32)
    bases = ((indices // N_FRONT) // 2) * 2 * front_seps
    slot_index = jnp.arange(P_SIZE, dtype=jnp.int32)

    def add_device(summed, pieces):
        off_one, forward_one, rows_one, fill_one, base_one = pieces
        product = jnp.einsum('kpab,kbr->kpar', off_one.astype(jnp.float32), forward_one.astype(jnp.float32))
        used_slots = slot_index[None, :] < fill_one[:, None]
        product = jnp.where(used_slots[:, :, None, None], product, jnp.zeros((), jnp.float32))
        target = (base_one + rows_one).reshape(-1).astype(jnp.int32)
        summed = summed.at[target].add(product.reshape(-1, B, R))
        return summed, None

    summed, _ = lax.scan(add_device, jnp.zeros((N_LEAF * front_seps, B, R), jnp.float32),
                         (off_dev, forward, rows_dev, fill_dev, bases))
    separator_in = (sep_rhs.astype(jnp.float32) - summed).astype(jnp.bfloat16)
    slot_rows = sep_inverse.reshape(N_LEAF, front_seps, B, front_seps * B)

    def to_natural(slot_block, order_row):
        return jnp.zeros_like(slot_block).at[order_row].set(slot_block)

    natural = jax.vmap(to_natural)(slot_rows, panel_order)

    def solve_front(pieces):
        matrix, rhs_group = pieces
        matrix = matrix.reshape(front_seps * B, front_seps * B)
        flat = rhs_group.reshape(front_seps * B, R)
        solved_forward = jnp.dot(matrix, flat, preferred_element_type=jnp.float32).astype(jnp.bfloat16)
        adjoint_out = jnp.dot(matrix.T, solved_forward, preferred_element_type=jnp.float32)
        return solved_forward, adjoint_out

    sep_fwd, sep_adj = lax.map(solve_front, (natural, separator_in.reshape(N_LEAF, front_seps, B, R)))
    sep_forward = sep_fwd.reshape(N_LEAF * front_seps, B, R)
    sep_solution = sep_adj.reshape(N_LEAF * front_seps, B, R)
    solved = sep_solution.astype(jnp.bfloat16)

    def back_device(pieces):
        inverse_one, off_one, forward_one, rows_one, fill_one, base_one = pieces
        picked = solved[(base_one + rows_one).astype(jnp.int32)]
        used_slots = slot_index[None, :] < fill_one[:, None]
        picked = jnp.where(used_slots[:, :, None, None], picked, jnp.zeros((), jnp.bfloat16))
        pulled = jnp.einsum('kpab,kpar->kbr', off_one.astype(jnp.float32), picked.astype(jnp.float32))
        backward = (forward_one.astype(jnp.float32) - pulled).astype(jnp.bfloat16)
        return jnp.einsum('kba,kbr->kar', inverse_one.astype(jnp.float32), backward.astype(jnp.float32)).astype(jnp.bfloat16)

    leaf_out = lax.map(back_device, (inverse_dev, off_dev, forward, rows_dev, fill_dev, bases))
    return leaf_out.reshape(devices * K_DEV, B, R), sep_forward, sep_solution
```

```python
import functools

import jax
import jax.numpy as jnp
from jax import lax
from jax.experimental import pallas as pl
from jax.experimental.pallas import tpu as pltpu
from jax.sharding import PartitionSpec as P

X = 4
F32 = jnp.float32
BF16 = jnp.bfloat16


def groups(fronts):
    rows = fronts // X
    along_x = [[z * X + x for x in range(X)] for z in range(rows)]
    along_z = [[z * X + x for z in range(rows)] for x in range(X)]
    return along_x, along_z


def exchange(value, where):
    return lax.all_to_all(value, "front", 0, 0, tiled=True, axis_index_groups=where)


def sibling(value):
    size = lax.axis_size("leaf")
    return lax.ppermute(value, "leaf", [(i, i ^ 1) for i in range(size)])


def place(row, parity, seps):
    rows = seps // X
    local = lax.rem(row, seps)
    half = row // seps
    own = lax.rem(local, X) * rows + local // X
    return jnp.where(half == parity, own, own + seps)


def forward_kernel(per, slots, seps, rows_ref, fill_ref, parity_ref, inv_ref, rhs_ref, off_ref,
                   fwd_ref, out_ref, acc):
    step = pl.program_id(0)
    parity = parity_ref[0]

    @pl.when(step == 0)
    def _():
        acc[...] = jnp.zeros_like(acc)

    for k in range(per):
        leaf = step * per + k
        fwd = jnp.dot(inv_ref[k], rhs_ref[k], preferred_element_type=F32).astype(BF16)
        fwd_ref[k] = fwd
        fill = fill_ref[leaf]
        for p in range(slots):
            product = jnp.dot(off_ref[k, p], fwd, preferred_element_type=F32)
            spot = place(rows_ref[leaf * slots + p], parity, seps)
            spot = jnp.where(p < fill, spot, 2 * seps)
            acc[spot] += product

    @pl.when(step == pl.num_programs(0) - 1)
    def _():
        def body(i, _):
            out_ref[i] = acc[i].astype(BF16)
            return 0
        lax.fori_loop(0, 2 * seps, body, 0)


def forward_leaves(block_rows, fill_count, parity, leaf_inverse, leaf_rhs, off_blocks, seps, per=4):
    leaves, b, r = leaf_rhs.shape
    slots = off_blocks.shape[1]
    grid_spec = pltpu.PrefetchScalarGridSpec(
        num_scalar_prefetch=3,
        grid=(leaves // per,),
        in_specs=[
            pl.BlockSpec((per, b, b), lambda i, *_: (i, 0, 0)),
            pl.BlockSpec((per, b, r), lambda i, *_: (i, 0, 0)),
            pl.BlockSpec((per, slots, b, b), lambda i, *_: (i, 0, 0, 0)),
        ],
        out_specs=[
            pl.BlockSpec((per, b, r), lambda i, *_: (i, 0, 0)),
            pl.BlockSpec((2 * seps, b, r), lambda i, *_: (0, 0, 0)),
        ],
        scratch_shapes=[pltpu.VMEM((2 * seps + 1, b, r), F32)],
    )
    return pl.pallas_call(
        functools.partial(forward_kernel, per, slots, seps),
        grid_spec=grid_spec,
        out_shape=[
            jax.ShapeDtypeStruct((leaves, b, r), BF16),
            jax.ShapeDtypeStruct((2 * seps, b, r), BF16),
        ],
        compiler_params=pltpu.CompilerParams(vmem_limit_bytes=40 << 20),
    )(block_rows.reshape(-1), fill_count, parity, leaf_inverse, leaf_rhs, off_blocks)


def backward_kernel(per, slots, seps, rows_ref, fill_ref, parity_ref, inv_ref, fwd_ref, off_ref,
                    own_ref, other_ref, out_ref, field):
    step = pl.program_id(0)
    parity = parity_ref[0]

    @pl.when(step == 0)
    def _():
        field[pl.ds(0, seps)] = own_ref[...]
        field[pl.ds(seps, seps)] = other_ref[...]
        field[2 * seps] = jnp.zeros(field.shape[1:], field.dtype)

    for k in range(per):
        leaf = step * per + k
        fill = fill_ref[leaf]
        total = fwd_ref[k].astype(F32)
        for p in range(slots):
            spot = place(rows_ref[leaf * slots + p], parity, seps)
            spot = jnp.where(p < fill, spot, 2 * seps)
            total -= lax.dot_general(off_ref[k, p], field[spot], (((0,), (0,)), ((), ())),
                                     preferred_element_type=F32)
        out_ref[k] = lax.dot_general(inv_ref[k], total.astype(BF16), (((0,), (0,)), ((), ())),
                                     preferred_element_type=F32).astype(BF16)


def backward_leaves(block_rows, fill_count, parity, leaf_inverse, forward, off_blocks, own, other, per=4):
    leaves, b, r = forward.shape
    slots = off_blocks.shape[1]
    seps = own.shape[0]
    grid_spec = pltpu.PrefetchScalarGridSpec(
        num_scalar_prefetch=3,
        grid=(leaves // per,),
        in_specs=[
            pl.BlockSpec((per, b, b), lambda i, *_: (i, 0, 0)),
            pl.BlockSpec((per, b, r), lambda i, *_: (i, 0, 0)),
            pl.BlockSpec((per, slots, b, b), lambda i, *_: (i, 0, 0, 0)),
            pl.BlockSpec((seps, b, r), lambda i, *_: (0, 0, 0)),
            pl.BlockSpec((seps, b, r), lambda i, *_: (0, 0, 0)),
        ],
        out_specs=pl.BlockSpec((per, b, r), lambda i, *_: (i, 0, 0)),
        scratch_shapes=[pltpu.VMEM((2 * seps + 1, b, r), BF16)],
    )
    return pl.pallas_call(
        functools.partial(backward_kernel, per, slots, seps),
        grid_spec=grid_spec,
        out_shape=jax.ShapeDtypeStruct((leaves, b, r), BF16),
        compiler_params=pltpu.CompilerParams(vmem_limit_bytes=40 << 20),
    )(block_rows.reshape(-1), fill_count, parity, leaf_inverse, forward, off_blocks, own, other)


def on_device(
    leaf_inverse, leaf_rhs, off_blocks, block_rows, fill_count, sep_rhs, panel_order, sep_inverse
):
    b = leaf_inverse.shape[1]
    r = leaf_rhs.shape[2]
    seps = lax.axis_size("front")
    rows = seps // X
    along_x, along_z = groups(seps)
    parity = (lax.axis_index("leaf") % 2).astype(jnp.int32).reshape(1)
    me = lax.axis_index("front")
    my_x, my_z = me % X, me // X

    with jax.named_scope("spread_panels"):
        panels = sep_inverse.reshape(b, rows, X, b).transpose(2, 0, 1, 3).reshape(X, b, rows * b)
        panels = exchange(panels, along_x).reshape(X * b, rows * b)

    with jax.named_scope("leaf_forward"):
        forward, terms = forward_leaves(
            block_rows, fill_count, parity, leaf_inverse, leaf_rhs, off_blocks, seps
        )
    with jax.named_scope("sum_terms"):
        mine = terms[:seps].astype(F32) + sibling(terms[seps:]).astype(F32)
        got = exchange(mine.astype(BF16), along_x).reshape(X, rows, b, r)
        column = got.astype(F32).sum(0).astype(BF16)
        got = exchange(column, along_z)
        summed = got.astype(F32).sum(0)
    with jax.named_scope("separators"):
        separator_in = (sep_rhs[0].astype(F32) - summed).astype(BF16)
        right = exchange(jnp.broadcast_to(separator_in[None], (rows, b, r)), along_z)
        part = jnp.dot(panels, right.reshape(rows * b, r), preferred_element_type=F32).astype(BF16)
        parts = exchange(jnp.broadcast_to(part[None], (X, X * b, r)).reshape(X * X * b, r), along_x)
        solved_rows = parts.reshape(X, X * b, r).astype(F32).sum(0).astype(BF16)
        adjoint = lax.dot_general(panels, solved_rows, (((0,), (0,)), ((), ())), preferred_element_type=F32)
        got = exchange(adjoint.reshape(rows, b, r).astype(BF16), along_z)
        sep_solution = got.astype(F32).sum(0)
    with jax.named_scope("order_rows"):
        held = lax.dynamic_slice_in_dim(panel_order[0], my_z * X, X)
        wanted = jnp.arange(rows, dtype=jnp.int32) * X + my_x
        chosen = held[None, :] == wanted[:, None]
        blocks = jnp.where(
            chosen[:, :, None, None], solved_rows.reshape(1, X, b, r), jnp.zeros((), BF16)
        ).astype(F32).sum(1).astype(BF16)
        sep_forward = lax.psum_scatter(
            blocks, "front", scatter_dimension=0, tiled=True, axis_index_groups=along_z
        )
    with jax.named_scope("spread_solution"):
        solved = sep_solution.astype(BF16)
        column = exchange(jnp.broadcast_to(solved[None], (rows, b, r)), along_z)
        own = exchange(jnp.broadcast_to(column[None], (X, rows, b, r)).reshape(seps, b, r), along_x)
        other = sibling(own)
    with jax.named_scope("leaf_backward"):
        leaf_solution = backward_leaves(
            block_rows, fill_count, parity, leaf_inverse, forward, off_blocks, own, other
        )
    return leaf_solution, sep_forward, sep_solution[None]


def solution(mesh):
    both = ("leaf", "front")
    return jax.shard_map(
        on_device,
        mesh=mesh,
        in_specs=(
            P(both, None, None),
            P(both, None, None),
            P(both, None, None, None),
            P(both, None),
            P(both),
            P(both, None, None),
            P("leaf", None),
            P(both, None, None),
        ),
        out_specs=(P(both, None, None), P(both, None, None), P(both, None, None)),
        check_vma=False,
    )
```

```python
import functools

import jax
import jax.numpy as jnp
from jax import lax
from jax.experimental import pallas as pl
from jax.experimental.pallas import tpu as pltpu
from jax.sharding import PartitionSpec as P

X = 4
F32 = jnp.float32
BF16 = jnp.bfloat16


def groups(fronts):
    rows = fronts // X
    along_x = [[z * X + x for x in range(X)] for z in range(rows)]
    along_z = [[z * X + x for z in range(rows)] for x in range(X)]
    return along_x, along_z


def exchange(value, where):
    return lax.all_to_all(value, "front", 0, 0, tiled=True, axis_index_groups=where)


def sibling(value):
    size = lax.axis_size("leaf")
    return lax.ppermute(value, "leaf", [(i, i ^ 1) for i in range(size)])


def place(row, here, seps):
    parity, my_x = here
    rows = seps // X
    local = lax.rem(row, seps)
    away = lax.rem(lax.rem(local, X) + X - my_x, X)
    own = away * rows + local // X
    return jnp.where(row // seps == parity, own, own + seps)


def position():
    return lax.rem(lax.axis_index("leaf"), 2), lax.rem(lax.axis_index("front"), X)


def forward_kernel(per, seps, rows_ref, fill_ref, inv_hbm, rhs_hbm, off_hbm,
                   fwd_hbm, far_own, near_own, far_sib, near_sib,
                   fwd_ref, inv_ref, off_ref, rhs_ref, acc, sems, out_sems):
    leaves, slots, b, _ = off_ref.shape
    rows = seps // X
    here = position()
    copies = []
    for chunk in range(leaves // per):
        some = pl.ds(chunk * per, per)
        copies.append([
            pltpu.make_async_copy(source.at[some], target.at[some], sems.at[chunk, i])
            for i, (source, target) in enumerate(
                ((inv_hbm, inv_ref), (rhs_hbm, rhs_ref), (off_hbm, off_ref)))
        ])
        for copy in copies[-1]:
            copy.start()
    acc[...] = jnp.zeros_like(acc)
    sent = []
    for chunk in range(leaves // per):
        for copy in copies[chunk]:
            copy.wait()
        some = range(chunk * per, chunk * per + per)
        solved = []
        for k in some:
            fwd = jnp.dot(inv_ref[k], rhs_ref[k], preferred_element_type=F32).astype(BF16)
            fwd_ref[k] = fwd
            solved.append(fwd)
        for k, fwd in zip(some, solved):
            products = jnp.dot(off_ref[k].reshape(slots * b, b), fwd, preferred_element_type=F32)
            for p in range(slots):
                spot = jnp.where(p < fill_ref[k], place(rows_ref[p, k], here, seps), 2 * seps)
                acc[spot] += products[p * b:(p + 1) * b]
        some = pl.ds(chunk * per, per)
        sent.append(pltpu.make_async_copy(fwd_ref.at[some], fwd_hbm.at[some], out_sems.at[chunk]))
        sent[-1].start()
    for base, far, near in ((seps, far_sib, near_sib), (0, far_own, near_own)):
        for away, target, spot in ((2, far, 0), (1, near, 0), (3, near, rows), (0, near, 2 * rows)):
            for i in range(rows):
                target[spot + i] = acc[base + away * rows + i].astype(BF16)
    for copy in sent:
        copy.wait()


def forward_leaves(block_rows, fill_count, leaf_inverse, leaf_rhs, off_blocks, seps, per=8):
    leaves, b, r = leaf_rhs.shape
    rows = seps // X
    scalars = pl.BlockSpec(memory_space=pltpu.SMEM)
    anywhere = pl.BlockSpec(memory_space=pl.ANY)
    near_by = pl.BlockSpec(memory_space=pltpu.VMEM)
    far = pltpu.VMEM((rows, b, r), BF16)
    near = pltpu.VMEM((seps - rows, b, r), BF16)
    return pl.pallas_call(
        functools.partial(forward_kernel, per, seps),
        in_specs=[scalars, scalars, anywhere, anywhere, anywhere],
        out_specs=[anywhere] + [near_by] * 4,
        out_shape=[jax.ShapeDtypeStruct((leaves, b, r), BF16), far, near, far, near],
        scratch_shapes=[
            pltpu.VMEM((leaves, b, r), BF16),
            pltpu.VMEM(leaf_inverse.shape, BF16),
            pltpu.VMEM(off_blocks.shape, BF16),
            pltpu.VMEM((leaves, b, r), BF16),
            pltpu.VMEM((2 * seps + 1, b, r), F32),
            pltpu.SemaphoreType.DMA((leaves // per, 3)),
            pltpu.SemaphoreType.DMA((leaves // per,)),
        ],
        compiler_params=pltpu.CompilerParams(vmem_limit_bytes=56 << 20),
    )(block_rows.T, fill_count, leaf_inverse, leaf_rhs, off_blocks)


def hold_kernel(per, *refs):
    count = len(refs) // 2
    sems = refs[-1]
    copies = []
    for i, (source, target) in enumerate(zip(refs[:count], refs[count:])):
        for chunk in range(source.shape[0] // per):
            some = pl.ds(chunk * per, per)
            copies.append(pltpu.make_async_copy(source.at[some], target.at[some], sems.at[i, chunk]))
            copies[-1].start()
    for copy in copies:
        copy.wait()


def hold(*values, per=8):
    anywhere = pl.BlockSpec(memory_space=pl.ANY)
    near_by = pl.BlockSpec(memory_space=pltpu.VMEM)
    return pl.pallas_call(
        functools.partial(hold_kernel, per),
        in_specs=[anywhere] * len(values),
        out_specs=[near_by] * len(values),
        out_shape=[pltpu.VMEM(value.shape, value.dtype) for value in values],
        scratch_shapes=[pltpu.SemaphoreType.DMA((len(values), values[0].shape[0] // per))],
        compiler_params=pltpu.CompilerParams(vmem_limit_bytes=48 << 20),
    )(*values)


def backward_kernel(per, seps, starts, *refs):
    rows_ref, fill_ref, fwd_ref, inv_ref, off_ref = refs[:5]
    pieces = refs[5:5 + len(starts)]
    out_hbm, field, out, sems, out_sems = refs[5 + len(starts):]
    leaves, slots, b, _ = off_ref.shape
    here = position()
    copies = [
        pltpu.make_async_copy(piece, field.at[pl.ds(start, piece.shape[0])], sems.at[i])
        for i, (start, piece) in enumerate(zip(starts, pieces))
    ]
    for copy in copies:
        copy.start()
    field[2 * seps] = jnp.zeros(field.shape[1:], field.dtype)
    for copy in copies:
        copy.wait()
    copies = []
    transposed = (((0,), (0,)), ((), ()))
    for chunk in range(leaves // per):
        some = range(chunk * per, chunk * per + per)
        totals = []
        for k in some:
            picked = jnp.concatenate([
                field[jnp.where(p < fill_ref[k], place(rows_ref[p, k], here, seps), 2 * seps)]
                for p in range(slots)
            ], axis=0)
            pulled = lax.dot_general(off_ref[k].reshape(slots * b, b), picked, transposed,
                                     preferred_element_type=F32)
            totals.append((fwd_ref[k].astype(F32) - pulled).astype(BF16))
        for k, total in zip(some, totals):
            out[k] = lax.dot_general(inv_ref[k], total, transposed, preferred_element_type=F32).astype(BF16)
        some = pl.ds(chunk * per, per)
        copies.append(pltpu.make_async_copy(out.at[some], out_hbm.at[some], out_sems.at[chunk]))
        copies[-1].start()
    for copy in copies:
        copy.wait()


def backward_leaves(block_rows, fill_count, forward, leaf_inverse, off_blocks, starts, pieces, seps, per=8):
    leaves, b, r = forward.shape
    scalars = pl.BlockSpec(memory_space=pltpu.SMEM)
    anywhere = pl.BlockSpec(memory_space=pl.ANY)
    near_by = pl.BlockSpec(memory_space=pltpu.VMEM)
    return pl.pallas_call(
        functools.partial(backward_kernel, per, seps, starts),
        in_specs=[scalars, scalars] + [near_by] * 3 + [anywhere] * len(pieces),
        out_specs=anywhere,
        out_shape=jax.ShapeDtypeStruct((leaves, b, r), BF16),
        scratch_shapes=[
            pltpu.VMEM((2 * seps + 1, b, r), BF16),
            pltpu.VMEM((leaves, b, r), BF16),
            pltpu.SemaphoreType.DMA((len(pieces),)),
            pltpu.SemaphoreType.DMA((leaves // per,)),
        ],
        compiler_params=pltpu.CompilerParams(vmem_limit_bytes=28 << 20),
    )(block_rows.T, fill_count, forward, leaf_inverse, off_blocks, *pieces)


def shifted(value, by, fronts):
    return lax.ppermute(value, "front", [(i, i // X * X + (i + by) % X) for i in range(fronts)])


def added(*values):
    return sum(v.astype(F32) for v in values)


def local(kernel, outs, *values):
    near_by = pl.BlockSpec(memory_space=pltpu.VMEM)
    return pl.pallas_call(
        kernel,
        in_specs=[near_by] * len(values),
        out_specs=[near_by] * len(outs),
        out_shape=[jax.ShapeDtypeStruct(shape, BF16) for shape in outs],
    )(*values)


def split_kernel(panel_ref, *out_refs):
    b = panel_ref.shape[1]
    my_x = lax.rem(lax.axis_index("front"), X)
    for k, out in enumerate(out_refs):
        column = lax.rem(my_x + k, X)
        for z in range(out.shape[1] // b):
            start = pl.multiple_of((z * X + column) * b, b)
            out[:, z * b:(z + 1) * b] = panel_ref[0, :, pl.ds(start, b)]


def join_kernel(p0, p1, p2, p3, out_ref):
    b = p0.shape[0]
    my_x = lax.rem(lax.axis_index("front"), X)
    for k, panel in enumerate((p0, p1, p2, p3)):
        start = pl.multiple_of(lax.rem(my_x + X - k, X) * b, b)
        out_ref[pl.ds(start, b), :] = panel[...]


def on_device(
    leaf_inverse, leaf_rhs, off_blocks, block_rows, fill_count, sep_rhs, panel_order, sep_inverse
):
    b = leaf_inverse.shape[1]
    r = leaf_rhs.shape[2]
    seps = lax.axis_size("front")
    rows = seps // X
    half = rows // 2
    along_x, along_z = groups(seps)
    me = lax.axis_index("front")
    my_x, my_z = me % X, me // X
    shift = functools.partial(shifted, fronts=seps)
    together = lax.optimization_barrier

    with jax.named_scope("leaf_forward"):
        forward, far, near, far_sib, near_sib = forward_leaves(
            block_rows, fill_count, leaf_inverse, leaf_rhs, off_blocks, seps
        )
    with jax.named_scope("sum_terms"):
        far_in = sibling(far_sib)
        far_in, near_sib = together((far_in, near_sib))
        near_in = sibling(near_sib)
        right2 = shift(added(far[:half], far_in[:half]).astype(BF16), 1)
        left2 = shift(added(far[half:], far_in[half:]).astype(BF16), -1)

        def own(at):
            return added(near[at:at + rows], near_in[at:at + rows])

        none = ((0, 0), (0, 0))
        right2 = jnp.pad(right2.astype(F32), ((0, half), *none))
        left2 = jnp.pad(left2.astype(F32), ((half, 0), *none))
        from_left = shift((own(0) + right2).astype(BF16), 1)
        from_right = shift((own(rows) + left2).astype(BF16), -1)
        column = (own(2 * rows) + added(from_left, from_right)).astype(BF16)
    with jax.named_scope("spread_panels"):
        far_in, sep_inverse = together((far_in, sep_inverse))
        panels = list(local(split_kernel, [(b, rows * b)] * X, sep_inverse))
        panels[1], panels[3], column = together((panels[1], panels[3], column))
        panels[1], panels[3] = shift(panels[1], 1), shift(panels[3], -1)
    with jax.named_scope("sum_terms"):
        column = exchange(column, along_z)
        column, *panels = together((column, *panels))
        summed = added(*column)
    with jax.named_scope("spread_panels"):
        panels[2] = shift(panels[2], 2)
        (panel,) = local(join_kernel, [(X * b, rows * b)], *panels)
    with jax.named_scope("separators"):
        separator_in = (sep_rhs[0].astype(F32) - summed).astype(BF16)
        right = exchange(jnp.broadcast_to(separator_in[None], (rows, b, r)), along_z)
        part = jnp.dot(panel, right.reshape(rows * b, r), preferred_element_type=F32).astype(BF16)
        parts = exchange(jnp.broadcast_to(part[None], (X, X * b, r)).reshape(X * X * b, r), along_x)
        solved_rows = added(*parts.reshape(X, X * b, r)).astype(BF16)
        adjoint = lax.dot_general(panel, solved_rows, (((0,), (0,)), ((), ())), preferred_element_type=F32)
        sep_solution = added(*exchange(adjoint.reshape(rows, b, r).astype(BF16), along_z))
    with jax.named_scope("order_rows"):
        held = lax.dynamic_slice_in_dim(panel_order[0], my_z * X, X)
        wanted = jnp.arange(rows, dtype=jnp.int32) * X + my_x
        chosen = held[None, :] == wanted[:, None]
        blocks = jnp.where(
            chosen[:, :, None, None], solved_rows.reshape(1, X, b, r), jnp.zeros((), BF16)
        ).astype(F32).sum(1).astype(BF16)
    with jax.named_scope("spread_solution"):
        solved = sep_solution.astype(BF16)
        column = exchange(jnp.broadcast_to(solved[None], (rows, b, r)), along_z)
        slot = jnp.argmax(panel_order[0] == me).astype(jnp.int32)
        column, blocks, slot = together((column, blocks, slot))
        behind, ahead = shift(column, 1), shift(column, -1)
        far_low, far_high = shift(behind[:half], 1), shift(ahead[half:], -1)
    with jax.named_scope("order_rows"):
        blocks = exchange(blocks, along_z)
        far_low, far_high, blocks = together((far_low, far_high, blocks))
        sep_forward = lax.dynamic_slice_in_dim(blocks, slot // X, 1)
    with jax.named_scope("leaf_backward"):
        field = jnp.concatenate([column, ahead, far_low, far_high, behind])
        field, *leaves = together((field, forward, leaf_inverse, off_blocks))
        other = sibling(field)
        leaf_solution = backward_leaves(
            block_rows, fill_count, *hold(*leaves), [0, seps], [field, other], seps
        )
    return leaf_solution, sep_forward, sep_solution[None]


def solution(mesh):
    both = ("leaf", "front")
    return jax.shard_map(
        on_device,
        mesh=mesh,
        in_specs=(
            P(both, None, None),
            P(both, None, None),
            P(both, None, None, None),
            P(both, None),
            P(both),
            P(both, None, None),
            P("leaf", None),
            P(both, None, None),
        ),
        out_specs=(P(both, None, None), P(both, None, None), P(both, None, None)),
        check_vma=False,
    )
```

```python
import functools

import jax
import jax.numpy as jnp
from jax import lax
from jax.experimental import pallas as pl
from jax.experimental.pallas import tpu as pltpu
from jax.sharding import PartitionSpec as P

X = 4
F32 = jnp.float32
BF16 = jnp.bfloat16


def groups(fronts):
    rows = fronts // X
    along_x = [[z * X + x for x in range(X)] for z in range(rows)]
    along_z = [[z * X + x for z in range(rows)] for x in range(X)]
    return along_x, along_z


def exchange(value, where):
    return lax.all_to_all(value, "front", 0, 0, tiled=True, axis_index_groups=where)


def sibling(value):
    size = lax.axis_size("leaf")
    return lax.ppermute(value, "leaf", [(i, i ^ 1) for i in range(size)])


def place(row, here, seps):
    parity, my_x = here
    rows = seps // X
    local = lax.rem(row, seps)
    away = lax.rem(lax.rem(local, X) + X - my_x, X)
    own = away * rows + local // X
    return jnp.where(row // seps == parity, own, own + seps)


def position():
    return lax.rem(lax.axis_index("leaf"), 2), lax.rem(lax.axis_index("front"), X)


def forward_kernel(per, seps, rows_ref, fill_ref, inv_hbm, rhs_hbm, off_hbm,
                   fwd_hbm, far_own, near_own, far_sib, near_sib,
                   fwd_ref, inv_ref, off_ref, rhs_ref, acc, sems, out_sems):
    leaves, slots, b, _ = off_ref.shape
    rows = seps // X
    here = position()
    copies = []
    for chunk in range(leaves // per):
        some = pl.ds(chunk * per, per)
        copies.append([
            pltpu.make_async_copy(source.at[some], target.at[some], sems.at[chunk, i])
            for i, (source, target) in enumerate(
                ((inv_hbm, inv_ref), (rhs_hbm, rhs_ref), (off_hbm, off_ref)))
        ])
        for copy in copies[-1]:
            copy.start()
    acc[...] = jnp.zeros_like(acc)
    sent = []
    for chunk in range(leaves // per):
        for copy in copies[chunk]:
            copy.wait()
        some = range(chunk * per, chunk * per + per)
        solved = []
        for k in some:
            fwd = jnp.dot(inv_ref[k], rhs_ref[k], preferred_element_type=F32).astype(BF16)
            fwd_ref[k] = fwd
            solved.append(fwd)
        for k, fwd in zip(some, solved):
            products = jnp.dot(off_ref[k].reshape(slots * b, b), fwd, preferred_element_type=F32)
            for p in range(slots):
                spot = jnp.where(p < fill_ref[k], place(rows_ref[p, k], here, seps), 2 * seps)
                acc[spot] += products[p * b:(p + 1) * b]
        some = pl.ds(chunk * per, per)
        sent.append(pltpu.make_async_copy(fwd_ref.at[some], fwd_hbm.at[some], out_sems.at[chunk]))
        sent[-1].start()
    for base, far, near in ((seps, far_sib, near_sib), (0, far_own, near_own)):
        for away, target, spot in ((2, far, 0), (1, near, 0), (3, near, rows), (0, near, 2 * rows)):
            for i in range(rows):
                target[spot + i] = acc[base + away * rows + i].astype(BF16)
    for copy in sent:
        copy.wait()


def forward_leaves(block_rows, fill_count, leaf_inverse, leaf_rhs, off_blocks, seps, per=8):
    leaves, b, r = leaf_rhs.shape
    rows = seps // X
    scalars = pl.BlockSpec(memory_space=pltpu.SMEM)
    anywhere = pl.BlockSpec(memory_space=pl.ANY)
    near_by = pl.BlockSpec(memory_space=pltpu.VMEM)
    far = pltpu.VMEM((rows, b, r), BF16)
    near = pltpu.VMEM((seps - rows, b, r), BF16)
    return pl.pallas_call(
        functools.partial(forward_kernel, per, seps),
        in_specs=[scalars, scalars, anywhere, anywhere, anywhere],
        out_specs=[anywhere] + [near_by] * 4,
        out_shape=[jax.ShapeDtypeStruct((leaves, b, r), BF16), far, near, far, near],
        scratch_shapes=[
            pltpu.VMEM((leaves, b, r), BF16),
            pltpu.VMEM(leaf_inverse.shape, BF16),
            pltpu.VMEM(off_blocks.shape, BF16),
            pltpu.VMEM((leaves, b, r), BF16),
            pltpu.VMEM((2 * seps + 1, b, r), F32),
            pltpu.SemaphoreType.DMA((leaves // per, 3)),
            pltpu.SemaphoreType.DMA((leaves // per,)),
        ],
        compiler_params=pltpu.CompilerParams(vmem_limit_bytes=56 << 20),
    )(block_rows.T, fill_count, leaf_inverse, leaf_rhs, off_blocks)


def hold_kernel(per, order_ref, blocks, *refs):
    count = (len(refs) - 3) // 2
    rows_out, sems, row_sem = refs[-3:]
    copies = []
    for i, (source, target) in enumerate(zip(refs[:count], refs[count:])):
        for chunk in range(source.shape[0] // per):
            some = pl.ds(chunk * per, per)
            copies.append(pltpu.make_async_copy(source.at[some], target.at[some], sems.at[i, chunk]))
            copies[-1].start()
    me = lax.axis_index("front")
    holder = jnp.int32(0)
    for slot in range(order_ref.shape[1]):
        holder = jnp.where(order_ref[0, slot] == me, slot // X, holder)
    copies.append(pltpu.make_async_copy(blocks.at[pl.ds(holder, 1)], rows_out, row_sem))
    copies[-1].start()
    for copy in copies:
        copy.wait()


def hold(order, blocks, *values, per=8):
    anywhere = pl.BlockSpec(memory_space=pl.ANY)
    near_by = pl.BlockSpec(memory_space=pltpu.VMEM)
    return pl.pallas_call(
        functools.partial(hold_kernel, per),
        in_specs=[pl.BlockSpec(memory_space=pltpu.SMEM)] + [anywhere] * (1 + len(values)),
        out_specs=[near_by] * len(values) + [anywhere],
        out_shape=[pltpu.VMEM(value.shape, value.dtype) for value in values]
        + [jax.ShapeDtypeStruct((1, *blocks.shape[1:]), blocks.dtype)],
        scratch_shapes=[
            pltpu.SemaphoreType.DMA((len(values), values[0].shape[0] // per)),
            pltpu.SemaphoreType.DMA,
        ],
        compiler_params=pltpu.CompilerParams(vmem_limit_bytes=48 << 20),
    )(order, blocks, *values)


def backward_kernel(per, seps, starts, *refs):
    rows_ref, fill_ref, fwd_ref, inv_ref, off_ref = refs[:5]
    pieces = refs[5:5 + len(starts)]
    out_hbm, field, out, sems, out_sems = refs[5 + len(starts):]
    leaves, slots, b, _ = off_ref.shape
    here = position()
    copies = [
        pltpu.make_async_copy(piece, field.at[pl.ds(start, piece.shape[0])], sems.at[i])
        for i, (start, piece) in enumerate(zip(starts, pieces))
    ]
    for copy in copies:
        copy.start()
    field[2 * seps] = jnp.zeros(field.shape[1:], field.dtype)
    for copy in copies:
        copy.wait()
    copies = []
    transposed = (((0,), (0,)), ((), ()))
    for chunk in range(leaves // per):
        some = range(chunk * per, chunk * per + per)
        totals = []
        for k in some:
            picked = jnp.concatenate([
                field[jnp.where(p < fill_ref[k], place(rows_ref[p, k], here, seps), 2 * seps)]
                for p in range(slots)
            ], axis=0)
            pulled = lax.dot_general(off_ref[k].reshape(slots * b, b), picked, transposed,
                                     preferred_element_type=F32)
            totals.append((fwd_ref[k].astype(F32) - pulled).astype(BF16))
        for k, total in zip(some, totals):
            out[k] = lax.dot_general(inv_ref[k], total, transposed, preferred_element_type=F32).astype(BF16)
        some = pl.ds(chunk * per, per)
        copies.append(pltpu.make_async_copy(out.at[some], out_hbm.at[some], out_sems.at[chunk]))
        copies[-1].start()
    for copy in copies:
        copy.wait()


def backward_leaves(block_rows, fill_count, forward, leaf_inverse, off_blocks, starts, pieces, seps, per=8):
    leaves, b, r = forward.shape
    scalars = pl.BlockSpec(memory_space=pltpu.SMEM)
    anywhere = pl.BlockSpec(memory_space=pl.ANY)
    near_by = pl.BlockSpec(memory_space=pltpu.VMEM)
    return pl.pallas_call(
        functools.partial(backward_kernel, per, seps, starts),
        in_specs=[scalars, scalars] + [near_by] * 3 + [anywhere] * len(pieces),
        out_specs=anywhere,
        out_shape=jax.ShapeDtypeStruct((leaves, b, r), BF16),
        scratch_shapes=[
            pltpu.VMEM((2 * seps + 1, b, r), BF16),
            pltpu.VMEM((leaves, b, r), BF16),
            pltpu.SemaphoreType.DMA((len(pieces),)),
            pltpu.SemaphoreType.DMA((leaves // per,)),
        ],
        compiler_params=pltpu.CompilerParams(vmem_limit_bytes=28 << 20),
    )(block_rows.T, fill_count, forward, leaf_inverse, off_blocks, *pieces)


def shifted(value, by, fronts):
    return lax.ppermute(value, "front", [(i, i // X * X + (i + by) % X) for i in range(fronts)])


def added(*values):
    return sum(v.astype(F32) for v in values)


def local(kernel, outs, *values):
    near_by = pl.BlockSpec(memory_space=pltpu.VMEM)
    return pl.pallas_call(
        kernel,
        in_specs=[near_by] * len(values),
        out_specs=[near_by] * len(outs),
        out_shape=[jax.ShapeDtypeStruct(shape, BF16) for shape in outs],
    )(*values)


def split_kernel(panel_ref, *out_refs):
    b = panel_ref.shape[1]
    my_x = lax.rem(lax.axis_index("front"), X)
    for k, out in enumerate(out_refs):
        column = lax.rem(my_x + k, X)
        for z in range(out.shape[1] // b):
            start = pl.multiple_of((z * X + column) * b, b)
            out[:, z * b:(z + 1) * b] = panel_ref[0, :, pl.ds(start, b)]


def join_kernel(p0, p1, p2, p3, out_ref):
    b = p0.shape[0]
    my_x = lax.rem(lax.axis_index("front"), X)
    for k, panel in enumerate((p0, p1, p2, p3)):
        start = pl.multiple_of(lax.rem(my_x + X - k, X) * b, b)
        out_ref[pl.ds(start, b), :] = panel[...]


def on_device(
    leaf_inverse, leaf_rhs, off_blocks, block_rows, fill_count, sep_rhs, panel_order, sep_inverse
):
    b = leaf_inverse.shape[1]
    r = leaf_rhs.shape[2]
    seps = lax.axis_size("front")
    rows = seps // X
    half = rows // 2
    along_x, along_z = groups(seps)
    me = lax.axis_index("front")
    my_x, my_z = me % X, me // X
    shift = functools.partial(shifted, fronts=seps)
    together = lax.optimization_barrier

    with jax.named_scope("leaf_forward"):
        forward, far, near, far_sib, near_sib = forward_leaves(
            block_rows, fill_count, leaf_inverse, leaf_rhs, off_blocks, seps
        )
    with jax.named_scope("sum_terms"):
        far_in = sibling(far_sib)
        far_in, near_sib = together((far_in, near_sib))
        near_in = sibling(near_sib)
        right2 = shift(added(far[:half], far_in[:half]).astype(BF16), 1)
        left2 = shift(added(far[half:], far_in[half:]).astype(BF16), -1)

        def own(at):
            return added(near[at:at + rows], near_in[at:at + rows])

        none = ((0, 0), (0, 0))
        right2 = jnp.pad(right2.astype(F32), ((0, half), *none))
        left2 = jnp.pad(left2.astype(F32), ((half, 0), *none))
        from_left = shift((own(0) + right2).astype(BF16), 1)
        from_right = shift((own(rows) + left2).astype(BF16), -1)
        column = (own(2 * rows) + added(from_left, from_right)).astype(BF16)
    with jax.named_scope("spread_panels"):
        far_in, sep_inverse = together((far_in, sep_inverse))
        panels = list(local(split_kernel, [(b, rows * b)] * X, sep_inverse))
        panels[1], panels[3], column = together((panels[1], panels[3], column))
        panels[1], panels[3] = shift(panels[1], 1), shift(panels[3], -1)
    with jax.named_scope("sum_terms"):
        column = exchange(column, along_z)
        column, *panels = together((column, *panels))
        summed = added(*column)
    with jax.named_scope("spread_panels"):
        panels[2] = shift(panels[2], 2)
        (panel,) = local(join_kernel, [(X * b, rows * b)], *panels)
    with jax.named_scope("separators"):
        separator_in = (sep_rhs[0].astype(F32) - summed).astype(BF16)
        right = exchange(jnp.broadcast_to(separator_in[None], (rows, b, r)), along_z)
        part = jnp.dot(panel, right.reshape(rows * b, r), preferred_element_type=F32).astype(BF16)
        parts = exchange(jnp.broadcast_to(part[None], (X, X * b, r)).reshape(X * X * b, r), along_x)
        solved_rows = added(*parts.reshape(X, X * b, r)).astype(BF16)
        adjoint = lax.dot_general(panel, solved_rows, (((0,), (0,)), ((), ())), preferred_element_type=F32)
        sep_solution = added(*exchange(adjoint.reshape(rows, b, r).astype(BF16), along_z))
    with jax.named_scope("order_rows"):
        held = lax.dynamic_slice_in_dim(panel_order[0], my_z * X, X)
        wanted = jnp.arange(rows, dtype=jnp.int32) * X + my_x
        chosen = held[None, :] == wanted[:, None]
        blocks = jnp.where(
            chosen[:, :, None, None], solved_rows.reshape(1, X, b, r), jnp.zeros((), BF16)
        ).astype(F32).sum(1).astype(BF16)
    with jax.named_scope("spread_solution"):
        solved = sep_solution.astype(BF16)
        column = exchange(jnp.broadcast_to(solved[None], (rows, b, r)), along_z)
        column, blocks = together((column, blocks))
        behind, ahead = shift(column, 1), shift(column, -1)
        far_low, far_high = shift(behind[:half], 1), shift(ahead[half:], -1)
    with jax.named_scope("order_rows"):
        blocks = exchange(blocks, along_z)
        far_low, far_high, blocks = together((far_low, far_high, blocks))
    with jax.named_scope("leaf_backward"):
        field = jnp.concatenate([column, ahead, far_low, far_high, behind])
        field, *leaves = together((field, forward, leaf_inverse, off_blocks))
        other = sibling(field)
        *leaves, sep_forward = hold(panel_order, blocks, *leaves)
        leaf_solution = backward_leaves(
            block_rows, fill_count, *leaves, [0, seps], [field, other], seps
        )
    return leaf_solution, sep_forward, sep_solution[None]


def solution(mesh):
    both = ("leaf", "front")
    return jax.shard_map(
        on_device,
        mesh=mesh,
        in_specs=(
            P(both, None, None),
            P(both, None, None),
            P(both, None, None, None),
            P(both, None),
            P(both),
            P(both, None, None),
            P("leaf", None),
            P(both, None, None),
        ),
        out_specs=(P(both, None, None), P(both, None, None), P(both, None, None)),
        check_vma=False,
    )
```

```python
import functools

import jax
import jax.numpy as jnp
from jax import lax
from jax.experimental import pallas as pl
from jax.experimental.pallas import tpu as pltpu
from jax.sharding import PartitionSpec as P

X = 4
F32 = jnp.float32
BF16 = jnp.bfloat16


def groups(fronts):
    rows = fronts // X
    along_x = [[z * X + x for x in range(X)] for z in range(rows)]
    along_z = [[z * X + x for z in range(rows)] for x in range(X)]
    return along_x, along_z


def exchange(value, where):
    return lax.all_to_all(value, "front", 0, 0, tiled=True, axis_index_groups=where)


def sibling(value):
    size = lax.axis_size("leaf")
    return lax.ppermute(value, "leaf", [(i, i ^ 1) for i in range(size)])


def place(row, here, seps):
    parity, my_x = here
    rows = seps // X
    local = lax.rem(row, seps)
    away = lax.rem(lax.rem(local, X) + X - my_x, X)
    own = away * rows + local // X
    return jnp.where(row // seps == parity, own, own + seps)


def position():
    return lax.rem(lax.axis_index("leaf"), 2), lax.rem(lax.axis_index("front"), X)


def forward_kernel(per, seps, rows_ref, fill_ref, inv_hbm, rhs_hbm, off_hbm,
                   fwd_hbm, far_own, near_own, far_sib, near_sib,
                   fwd_ref, inv_ref, off_ref, rhs_ref, acc, sems, out_sems):
    leaves, slots, b, _ = off_ref.shape
    rows = seps // X
    here = position()
    copies = []
    for chunk in range(leaves // per):
        some = pl.ds(chunk * per, per)
        copies.append([
            pltpu.make_async_copy(source.at[some], target.at[some], sems.at[chunk, i])
            for i, (source, target) in enumerate(
                ((inv_hbm, inv_ref), (rhs_hbm, rhs_ref), (off_hbm, off_ref)))
        ])
        for copy in copies[-1]:
            copy.start()
    acc[...] = jnp.zeros_like(acc)
    sent = []
    for chunk in range(leaves // per):
        for copy in copies[chunk]:
            copy.wait()
        some = range(chunk * per, chunk * per + per)
        solved = []
        for k in some:
            fwd = jnp.dot(inv_ref[k], rhs_ref[k], preferred_element_type=F32).astype(BF16)
            fwd_ref[k] = fwd
            solved.append(fwd)
        for k, fwd in zip(some, solved):
            products = jnp.dot(off_ref[k].reshape(slots * b, b), fwd, preferred_element_type=F32)
            for p in range(slots):
                spot = jnp.where(p < fill_ref[k], place(rows_ref[p, k], here, seps), 2 * seps)
                acc[spot] += products[p * b:(p + 1) * b]
        some = pl.ds(chunk * per, per)
        sent.append(pltpu.make_async_copy(fwd_ref.at[some], fwd_hbm.at[some], out_sems.at[chunk]))
        sent[-1].start()
    for base, far, near in ((seps, far_sib, near_sib), (0, far_own, near_own)):
        for away, target, spot in ((2, far, 0), (1, near, 0), (3, near, rows), (0, near, 2 * rows)):
            for i in range(rows):
                target[spot + i] = acc[base + away * rows + i].astype(BF16)
    for copy in sent:
        copy.wait()


def forward_leaves(block_rows, fill_count, leaf_inverse, leaf_rhs, off_blocks, seps, per=8):
    leaves, b, r = leaf_rhs.shape
    rows = seps // X
    scalars = pl.BlockSpec(memory_space=pltpu.SMEM)
    anywhere = pl.BlockSpec(memory_space=pl.ANY)
    near_by = pl.BlockSpec(memory_space=pltpu.VMEM)
    far = pltpu.VMEM((rows, b, r), BF16)
    near = pltpu.VMEM((seps - rows, b, r), BF16)
    return pl.pallas_call(
        functools.partial(forward_kernel, per, seps),
        in_specs=[scalars, scalars, anywhere, anywhere, anywhere],
        out_specs=[anywhere] + [near_by] * 4,
        out_shape=[jax.ShapeDtypeStruct((leaves, b, r), BF16), far, near, far, near],
        scratch_shapes=[
            pltpu.VMEM((leaves, b, r), BF16),
            pltpu.VMEM(leaf_inverse.shape, BF16),
            pltpu.VMEM(off_blocks.shape, BF16),
            pltpu.VMEM((leaves, b, r), BF16),
            pltpu.VMEM((2 * seps + 1, b, r), F32),
            pltpu.SemaphoreType.DMA((leaves // per, 3)),
            pltpu.SemaphoreType.DMA((leaves // per,)),
        ],
        compiler_params=pltpu.CompilerParams(vmem_limit_bytes=56 << 20),
    )(block_rows.T, fill_count, leaf_inverse, leaf_rhs, off_blocks)


def hold_kernel(per, order_ref, blocks, *refs):
    count = (len(refs) - 3) // 2
    rows_out, sems, row_sem = refs[-3:]
    copies = []
    for i, (source, target) in enumerate(zip(refs[:count], refs[count:])):
        for chunk in range(source.shape[0] // per):
            some = pl.ds(chunk * per, per)
            copies.append(pltpu.make_async_copy(source.at[some], target.at[some], sems.at[i, chunk]))
            copies[-1].start()
    me = lax.axis_index("front")
    holder = jnp.int32(0)
    for slot in range(order_ref.shape[1]):
        holder = jnp.where(order_ref[0, slot] == me, slot // X, holder)
    copies.append(pltpu.make_async_copy(blocks.at[pl.ds(holder, 1)], rows_out, row_sem))
    copies[-1].start()
    for copy in copies:
        copy.wait()


def hold(order, blocks, *values, per=8):
    anywhere = pl.BlockSpec(memory_space=pl.ANY)
    near_by = pl.BlockSpec(memory_space=pltpu.VMEM)
    return pl.pallas_call(
        functools.partial(hold_kernel, per),
        in_specs=[pl.BlockSpec(memory_space=pltpu.SMEM)] + [anywhere] * (1 + len(values)),
        out_specs=[near_by] * len(values) + [anywhere],
        out_shape=[pltpu.VMEM(value.shape, value.dtype) for value in values]
        + [jax.ShapeDtypeStruct((1, *blocks.shape[1:]), blocks.dtype)],
        scratch_shapes=[
            pltpu.SemaphoreType.DMA((len(values), values[0].shape[0] // per)),
            pltpu.SemaphoreType.DMA,
        ],
        compiler_params=pltpu.CompilerParams(vmem_limit_bytes=48 << 20),
    )(order, blocks, *values)


def backward_kernel(per, seps, starts, *refs):
    rows_ref, fill_ref, fwd_ref, inv_ref, off_ref = refs[:5]
    pieces = refs[5:5 + len(starts)]
    out_hbm, field, out, sems, out_sems = refs[5 + len(starts):]
    leaves, slots, b, _ = off_ref.shape
    here = position()
    copies = [
        pltpu.make_async_copy(piece, field.at[pl.ds(start, piece.shape[0])], sems.at[i])
        for i, (start, piece) in enumerate(zip(starts, pieces))
    ]
    for copy in copies:
        copy.start()
    field[2 * seps] = jnp.zeros(field.shape[1:], field.dtype)
    for copy in copies:
        copy.wait()
    copies = []
    transposed = (((0,), (0,)), ((), ()))
    for chunk in range(leaves // per):
        some = range(chunk * per, chunk * per + per)
        totals = []
        for k in some:
            picked = jnp.concatenate([
                field[jnp.where(p < fill_ref[k], place(rows_ref[p, k], here, seps), 2 * seps)]
                for p in range(slots)
            ], axis=0)
            pulled = lax.dot_general(off_ref[k].reshape(slots * b, b), picked, transposed,
                                     preferred_element_type=F32)
            totals.append((fwd_ref[k].astype(F32) - pulled).astype(BF16))
        for k, total in zip(some, totals):
            out[k] = lax.dot_general(inv_ref[k], total, transposed, preferred_element_type=F32).astype(BF16)
        some = pl.ds(chunk * per, per)
        copies.append(pltpu.make_async_copy(out.at[some], out_hbm.at[some], out_sems.at[chunk]))
        copies[-1].start()
    for copy in copies:
        copy.wait()


def backward_leaves(block_rows, fill_count, forward, leaf_inverse, off_blocks, starts, pieces, seps, per=8):
    leaves, b, r = forward.shape
    scalars = pl.BlockSpec(memory_space=pltpu.SMEM)
    anywhere = pl.BlockSpec(memory_space=pl.ANY)
    near_by = pl.BlockSpec(memory_space=pltpu.VMEM)
    return pl.pallas_call(
        functools.partial(backward_kernel, per, seps, starts),
        in_specs=[scalars, scalars] + [near_by] * 3 + [anywhere] * len(pieces),
        out_specs=anywhere,
        out_shape=jax.ShapeDtypeStruct((leaves, b, r), BF16),
        scratch_shapes=[
            pltpu.VMEM((2 * seps + 1, b, r), BF16),
            pltpu.VMEM((leaves, b, r), BF16),
            pltpu.SemaphoreType.DMA((len(pieces),)),
            pltpu.SemaphoreType.DMA((leaves // per,)),
        ],
        compiler_params=pltpu.CompilerParams(vmem_limit_bytes=28 << 20),
    )(block_rows.T, fill_count, forward, leaf_inverse, off_blocks, *pieces)


def shifted(value, by, fronts):
    return lax.ppermute(value, "front", [(i, i // X * X + (i + by) % X) for i in range(fronts)])


def added(*values):
    return sum(v.astype(F32) for v in values)


def local(kernel, outs, *values):
    near_by = pl.BlockSpec(memory_space=pltpu.VMEM)
    return pl.pallas_call(
        kernel,
        in_specs=[near_by] * len(values),
        out_specs=[near_by] * len(outs),
        out_shape=[jax.ShapeDtypeStruct(shape, BF16) for shape in outs],
    )(*values)


def split_kernel(panel_ref, *out_refs):
    b = panel_ref.shape[1]
    my_x = lax.rem(lax.axis_index("front"), X)
    for k, out in enumerate(out_refs):
        column = lax.rem(my_x + k, X)
        for z in range(out.shape[1] // b):
            start = pl.multiple_of((z * X + column) * b, b)
            out[:, z * b:(z + 1) * b] = panel_ref[0, :, pl.ds(start, b)]


def join_kernel(p0, p1, p2, p3, out_ref):
    b = p0.shape[0]
    my_x = lax.rem(lax.axis_index("front"), X)
    for k, panel in enumerate((p0, p1, p2, p3)):
        start = pl.multiple_of(lax.rem(my_x + X - k, X) * b, b)
        out_ref[pl.ds(start, b), :] = panel[...]


def on_device(
    leaf_inverse, leaf_rhs, off_blocks, block_rows, fill_count, sep_rhs, panel_order, sep_inverse
):
    b = leaf_inverse.shape[1]
    r = leaf_rhs.shape[2]
    seps = lax.axis_size("front")
    rows = seps // X
    half = rows // 2
    along_x, along_z = groups(seps)
    me = lax.axis_index("front")
    my_x, my_z = me % X, me // X
    shift = functools.partial(shifted, fronts=seps)
    together = lax.optimization_barrier

    with jax.named_scope("leaf_forward"):
        forward, far, near, far_sib, near_sib = forward_leaves(
            block_rows, fill_count, leaf_inverse, leaf_rhs, off_blocks, seps
        )
    with jax.named_scope("sum_terms"):
        far_in = sibling(far_sib)
        far_in, near_sib = together((far_in, near_sib))
        near_in = sibling(near_sib)
        right2 = shift(added(far[:half], far_in[:half]).astype(BF16), 1)
        left2 = shift(added(far[half:], far_in[half:]).astype(BF16), -1)

        def own(at):
            return added(near[at:at + rows], near_in[at:at + rows])

        none = ((0, 0), (0, 0))
        right2 = jnp.pad(right2.astype(F32), ((0, half), *none))
        left2 = jnp.pad(left2.astype(F32), ((half, 0), *none))
        from_left = shift((own(0) + right2).astype(BF16), 1)
        from_right = shift((own(rows) + left2).astype(BF16), -1)
        column = (own(2 * rows) + added(from_left, from_right)).astype(BF16)
    with jax.named_scope("spread_panels"):
        far_in, sep_inverse = together((far_in, sep_inverse))
        panels = list(local(split_kernel, [(b, rows * b)] * X, sep_inverse))
        panels[1], panels[3], column = together((panels[1], panels[3], column))
        panels[1], panels[3] = shift(panels[1], 1), shift(panels[3], -1)
    with jax.named_scope("sum_terms"):
        column = exchange(column, along_z)
        column, *panels = together((column, *panels))
        summed = added(*column)
    with jax.named_scope("spread_panels"):
        panels[2] = shift(panels[2], 2)
        (panel,) = local(join_kernel, [(X * b, rows * b)], *panels)
    with jax.named_scope("separators"):
        separator_in = (sep_rhs[0].astype(F32) - summed).astype(BF16)
        right = exchange(jnp.broadcast_to(separator_in[None], (rows, b, r)), along_z)
        part = jnp.dot(panel, right.reshape(rows * b, r), preferred_element_type=F32).astype(BF16)
        solved_rows = added(part, *(shift(part, by) for by in (2, 1, -1))).astype(BF16)
        adjoint = lax.dot_general(panel, solved_rows, (((0,), (0,)), ((), ())), preferred_element_type=F32)
        sep_solution = added(*exchange(adjoint.reshape(rows, b, r).astype(BF16), along_z))
    with jax.named_scope("order_rows"):
        held = lax.dynamic_slice_in_dim(panel_order[0], my_z * X, X)
        wanted = jnp.arange(rows, dtype=jnp.int32) * X + my_x
        chosen = held[None, :] == wanted[:, None]
        blocks = jnp.where(
            chosen[:, :, None, None], solved_rows.reshape(1, X, b, r), jnp.zeros((), BF16)
        ).astype(F32).sum(1).astype(BF16)
    with jax.named_scope("spread_solution"):
        solved = sep_solution.astype(BF16)
        column = exchange(jnp.broadcast_to(solved[None], (rows, b, r)), along_z)
        column, blocks = together((column, blocks))
        behind, ahead = shift(column, 1), shift(column, -1)
        far_low, far_high = shift(behind[:half], 1), shift(ahead[half:], -1)
    with jax.named_scope("order_rows"):
        blocks = exchange(blocks, along_z)
        far_low, far_high, blocks = together((far_low, far_high, blocks))
    with jax.named_scope("leaf_backward"):
        field = jnp.concatenate([column, ahead, far_low, far_high, behind])
        field, *leaves = together((field, forward, leaf_inverse, off_blocks))
        other = sibling(field)
        *leaves, sep_forward = hold(panel_order, blocks, *leaves)
        leaf_solution = backward_leaves(
            block_rows, fill_count, *leaves, [0, seps], [field, other], seps
        )
    return leaf_solution, sep_forward, sep_solution[None]


def solution(mesh):
    both = ("leaf", "front")
    return jax.shard_map(
        on_device,
        mesh=mesh,
        in_specs=(
            P(both, None, None),
            P(both, None, None),
            P(both, None, None, None),
            P(both, None),
            P(both),
            P(both, None, None),
            P("leaf", None),
            P(both, None, None),
        ),
        out_specs=(P(both, None, None), P(both, None, None), P(both, None, None)),
        check_vma=False,
    )
```
